32 devices in a mesh: groups: 2 (over x), docs: 16 (over z, y, core).
Axes of the slice: x: 2, y: 2, z: 4, core: 2. Of those that a mesh axis runs over, the one named last changes fastest.
Arguments:
- train_grads: bfloat16 [512, 32768], P('groups', 'docs'), parts along dimension 0, may hold values from -400 to 400, as said below
- query_grads: bfloat16 [600, 32768], P(None, 'docs'), may hold values from -400 to 400, as said below
Outputs:
- scores: float32 [512, 600], P(('groups', 'docs')), parts along dimension 0
The draws below stay inside these ranges and needn't reach their ends.
There are 2 independent parts, one for each index of `groups`. The reference program is written for one: setup_inputs(seed, part) draws one part's arguments, and reference() takes and returns one part's arrays. A program takes and returns all parts, laid end to end along the dimension named above; an argument that names none is the same for every part. Nothing has to cross between parts.
Inputs may be any that keep to these rules, and one draw needn't show every extreme that they name: `train_grads`: finite real values. `query_grads`: finite real values.
All inputs are finite; a program needn't handle non-finite values.
Results may differ from the reference program's by a relative error of at most 0.0003.
Values sent between devices are 32-bit elements; how exact they have to be, the bound alone decides.
No kernel may reach another device: no remote copies, remote signals or barrier semaphores. Data moves between devices by JAX's collectives and lax.ppermute only.
A program may use at most 64 MiB of HBM per device.

```python
import math
import jax
import jax.numpy as jnp
from jax import lax

LAYER_DIM = 4096
QUERIES = 600
DOCS = 256
LAYERS = 8
PROJ = 32768


def scaled_field(key, rows, cols, row_top):
    first, second, third = jax.random.split(key, 3)
    noise = jax.random.truncated_normal(first, -4.0, 4.0, (rows, cols), jnp.float32)
    row_scale = jnp.exp(jax.random.uniform(second, (rows, 1), jnp.float32) * math.log(row_top))
    col_scale = jnp.exp(jax.random.uniform(third, (1, cols), jnp.float32) * math.log(10.0))
    return noise * row_scale * col_scale


def draw_train_grads(key, part):
    key = jax.random.fold_in(key, 11)
    values = scaled_field(key, DOCS, PROJ, 10.0)
    return values.astype(jnp.bfloat16)


def draw_query_grads(key, part):
    key = jax.random.fold_in(key, 23)
    values = scaled_field(key, QUERIES, PROJ, 10.0)
    return values.astype(jnp.bfloat16)


def setup_inputs(seed: int = 0, part: int = 0) -> dict:
    streams_of = jax.random.split(jax.random.key(seed), 3)
    part_splits = jax.random.split(jax.random.fold_in(streams_of[2], part), 3)
    return {
        "train_grads": draw_train_grads(jax.random.fold_in(jax.random.fold_in(streams_of[2], part), 71), part),
        "query_grads": draw_query_grads(jax.random.fold_in(streams_of[2], 71), part),
    }


def reference(train_grads, query_grads):
    eps = 1e-06

    def layer_step(layer, total):
        start = (jnp.asarray(layer).astype(jnp.int32) * LAYER_DIM).astype(jnp.int32)
        docs_part = lax.dynamic_slice_in_dim(train_grads, start, LAYER_DIM, 1)
        query_part = lax.dynamic_slice_in_dim(query_grads, start, LAYER_DIM, 1)
        doc_sq = lax.optimization_barrier(jnp.sum(jnp.square(docs_part.astype(jnp.float32)), axis=1))
        query_sq = lax.optimization_barrier(jnp.sum(jnp.square(query_part.astype(jnp.float32)), axis=1))
        dots = lax.dot_general(docs_part, query_part, (((1,), (1,)), ((), ())), preferred_element_type=jnp.float32)
        weight = lax.rsqrt(doc_sq + eps)[:, None] * lax.rsqrt(query_sq + eps)[None, :]
        return total + dots * weight
    total = lax.fori_loop(0, LAYERS, layer_step, jnp.zeros((DOCS, QUERIES), jnp.float32))
    return total * math.sqrt(LAYER_DIM / LAYERS)
```

```python
import functools
import math

import jax
import jax.numpy as jnp
from jax import lax
from jax.experimental import pallas as pl
from jax.experimental.pallas import tpu as pltpu
from jax.sharding import PartitionSpec as P

EPS = 1e-06
LANES = 128
CHUNKS = 4


def order(chips, core):
    masks = [1 << b for b in range(chips.bit_length() - 1)]
    if core == 0 and len(masks) > 1:
        masks[0], masks[1] = masks[1], masks[0]
    return masks


def relative(chips, core, slot):
    masks = order(chips, core)
    return sum(m for i, m in enumerate(reversed(masks)) if slot >> i & 1)


def partial_squares(x):
    total = None
    for start in range(0, x.shape[1], LANES):
        part = x[:, start : start + LANES].astype(jnp.float32)
        part = part * part
        total = part if total is None else total + part
    return total


def dots_kernel(chips, train, query, keep, send, train_v, query_v, acc, doc_part, query_part, sem):
    docs, width = train.shape
    queries = query.shape[0]
    rows = docs // (2 * chips)
    step = width // CHUNKS
    me = lax.axis_index("docs")
    core, chip = lax.rem(me, 2), lax.div(me, 2)
    copies = []
    for k in range(CHUNKS):
        cols = pl.ds(k * step, step)
        pair = [
            pltpu.make_async_copy(train.at[:, cols], train_v.at[k], sem.at[k, 0]),
            pltpu.make_async_copy(query.at[:, cols], query_v.at[k], sem.at[k, 1]),
        ]
        for copy in pair:
            copy.start()
        copies.append(pair)
    for k in range(CHUNKS):
        for copy in copies[k]:
            copy.wait()
        a, b = train_v[k], query_v[k]
        dots = lax.dot_general(a, b, (((1,), (1,)), ((), ())), preferred_element_type=jnp.float32)
        if k == 0:
            acc[:, :queries] = dots
            doc_part[...] = partial_squares(a)
            query_part[...] = partial_squares(b)
        else:
            acc[:, :queries] += dots
            doc_part[...] += partial_squares(a)
            query_part[...] += partial_squares(b)
    acc[:, queries : queries + 1] = jnp.sum(doc_part[...], axis=1, keepdims=True)
    query_row = jnp.sum(query_part[...].T, axis=0, keepdims=True)
    half = chips * rows
    for out, owner in ((keep, core), (send, 1 - core)):
        for slot in range(chips):
            rel = jnp.where(owner == 0, relative(chips, 0, slot), relative(chips, 1, slot))
            target = jnp.bitwise_xor(chip, rel)
            start = pl.multiple_of(target * (2 * rows) + owner * rows, rows)
            out[slot * rows : (slot + 1) * rows, : queries + 1] = acc[pl.ds(start, rows), : queries + 1]
        out[half : half + 1, :queries] = query_row


def scale_kernel(factor, queries, keep, got, terms):
    half = terms.shape[0]
    doc = lax.rsqrt(keep[:half, queries : queries + 1] + got[:half, queries : queries + 1] + EPS) * factor
    query = lax.rsqrt(keep[half : half + 1, :queries] + got[half : half + 1, :queries] + EPS)
    terms[...] = (keep[:half, :queries] + got[:half, :queries]) * doc * query


def local(train_grads, query_grads):
    devices = lax.axis_size("docs")
    chips = devices // 2
    docs, width = train_grads.shape
    queries = query_grads.shape[0]
    factor = math.sqrt(2 * width / chips)
    half = docs // 2
    padded = pl.cdiv(queries + 1, LANES) * LANES
    packed = jax.ShapeDtypeStruct((half + 8, padded), jnp.float32)
    step = width // CHUNKS
    keep, send = pl.pallas_call(
        functools.partial(dots_kernel, chips),
        out_shape=[packed, packed],
        in_specs=[pl.BlockSpec(memory_space=pl.ANY)] * 2,
        out_specs=[pl.BlockSpec(memory_space=pltpu.VMEM)] * 2,
        scratch_shapes=[
            pltpu.VMEM((CHUNKS, docs, step), jnp.bfloat16),
            pltpu.VMEM((CHUNKS, queries, step), jnp.bfloat16),
            pltpu.VMEM((docs, padded), jnp.float32),
            pltpu.VMEM((docs, LANES), jnp.float32),
            pltpu.VMEM((queries, LANES), jnp.float32),
            pltpu.SemaphoreType.DMA((CHUNKS, 2)),
        ],
        compiler_params=pltpu.CompilerParams(vmem_limit_bytes=40 * 2**20),
        name="dots",
    )(train_grads, query_grads)
    got = lax.ppermute(send, "docs", [(i, i ^ 1) for i in range(devices)])
    terms = pl.pallas_call(
        functools.partial(scale_kernel, factor, queries),
        out_shape=jax.ShapeDtypeStruct((half, queries), jnp.float32),
        compiler_params=pltpu.CompilerParams(vmem_limit_bytes=40 * 2**20),
        name="scale",
    )(keep, got)
    orders = order(chips, 0), order(chips, 1)
    for masks in zip(*orders):
        middle = terms.shape[0] // 2
        pairs = [(i, i ^ 2 * masks[i % 2]) for i in range(devices)]
        terms = terms[:middle] + lax.ppermute(terms[middle:], "docs", pairs)
    return terms


def solution(mesh):
    in_specs = (P("groups", "docs"), P(None, "docs"))
    out_specs = P(("groups", "docs"), None)
    return jax.shard_map(local, mesh=mesh, in_specs=in_specs, out_specs=out_specs, check_vma=False)
```

```python
import functools
import math

import jax
import jax.numpy as jnp
from jax import lax
from jax.experimental import pallas as pl
from jax.experimental.pallas import tpu as pltpu
from jax.sharding import PartitionSpec as P

EPS = 1e-06
LANES = 128
CHUNKS = 4


def phases(chips):
    bits = chips.bit_length() - 1
    pairs = [[0, 3 << b, 1 << b, 2 << b] for b in range(0, bits - 1, 2)]
    return pairs + [[0, 1 << bits - 1]] * (bits % 2)


def relative(chips, slot):
    total = 0
    for offsets in reversed(phases(chips)):
        slot, digit = divmod(slot, len(offsets))
        total ^= offsets[digit]
    return total


def partial_squares(x):
    total = None
    for start in range(0, x.shape[1], LANES):
        part = x[:, start : start + LANES].astype(jnp.float32)
        part = part * part
        total = part if total is None else total + part
    return total


def dots_kernel(chips, train, query, keep, send, train_v, query_v, acc, doc_part, query_part, sem):
    docs, width = train.shape
    queries = query.shape[0]
    rows = docs // (2 * chips)
    step = width // CHUNKS
    me = lax.axis_index("docs")
    core, chip = lax.rem(me, 2), lax.div(me, 2)
    copies = []
    for k in range(CHUNKS):
        cols = pl.ds(k * step, step)
        pair = [
            pltpu.make_async_copy(train.at[:, cols], train_v.at[k], sem.at[k, 0]),
            pltpu.make_async_copy(query.at[:, cols], query_v.at[k], sem.at[k, 1]),
        ]
        for copy in pair:
            copy.start()
        copies.append(pair)
    for k in range(CHUNKS):
        for copy in copies[k]:
            copy.wait()
        a, b = train_v[k], query_v[k]
        dots = lax.dot_general(a, b, (((1,), (1,)), ((), ())), preferred_element_type=jnp.float32)
        if k == 0:
            acc[:, :queries] = dots
            doc_part[...] = partial_squares(a)
            query_part[...] = partial_squares(b)
        else:
            acc[:, :queries] += dots
            doc_part[...] += partial_squares(a)
            query_part[...] += partial_squares(b)
    acc[:, queries : queries + 1] = jnp.sum(doc_part[...], axis=1, keepdims=True)
    query_row = jnp.sum(query_part[...].T, axis=0, keepdims=True)
    half = chips * rows
    for out, owner in ((keep, core), (send, 1 - core)):
        for slot in range(chips):
            target = jnp.bitwise_xor(chip, relative(chips, slot))
            start = pl.multiple_of(target * (2 * rows) + owner * rows, rows)
            out[slot * rows : (slot + 1) * rows, : queries + 1] = acc[pl.ds(start, rows), : queries + 1]
        out[half : half + 1, :queries] = query_row


def scale_kernel(factor, queries, keep, got, terms):
    half = terms.shape[0]
    doc = lax.rsqrt(keep[:half, queries : queries + 1] + got[:half, queries : queries + 1] + EPS) * factor
    query = lax.rsqrt(keep[half : half + 1, :queries] + got[half : half + 1, :queries] + EPS)
    terms[...] = (keep[:half, :queries] + got[:half, :queries]) * doc * query


def local(train_grads, query_grads):
    devices = lax.axis_size("docs")
    chips = devices // 2
    docs, width = train_grads.shape
    queries = query_grads.shape[0]
    factor = math.sqrt(2 * width / chips)
    half = docs // 2
    padded = pl.cdiv(queries + 1, LANES) * LANES
    packed = jax.ShapeDtypeStruct((half + 8, padded), jnp.float32)
    step = width // CHUNKS
    keep, send = pl.pallas_call(
        functools.partial(dots_kernel, chips),
        out_shape=[packed, packed],
        in_specs=[pl.BlockSpec(memory_space=pltpu.HBM)] * 2,
        out_specs=[pl.BlockSpec(memory_space=pltpu.VMEM)] * 2,
        scratch_shapes=[
            pltpu.VMEM((CHUNKS, docs, step), jnp.bfloat16),
            pltpu.VMEM((CHUNKS, queries, step), jnp.bfloat16),
            pltpu.VMEM((docs, padded), jnp.float32),
            pltpu.VMEM((docs, LANES), jnp.float32),
            pltpu.VMEM((queries, LANES), jnp.float32),
            pltpu.SemaphoreType.DMA((CHUNKS, 2)),
        ],
        compiler_params=pltpu.CompilerParams(vmem_limit_bytes=40 * 2**20),
        name="dots",
    )(*(pltpu.with_memory_space_constraint(x, pltpu.HBM) for x in (train_grads, query_grads)))
    got = lax.ppermute(send, "docs", [(i, i ^ 1) for i in range(devices)])
    terms = pl.pallas_call(
        functools.partial(scale_kernel, factor, queries),
        out_shape=jax.ShapeDtypeStruct((half, queries), jnp.float32),
        compiler_params=pltpu.CompilerParams(vmem_limit_bytes=40 * 2**20),
        name="scale",
    )(keep, got)
    for offsets in phases(chips):
        parts = jnp.split(terms, len(offsets))
        moves = [[(i, i ^ 2 * offset) for i in range(devices)] for offset in offsets]
        terms = parts[0]
        for part, pairs in zip(parts[1:], moves[1:]):
            terms = terms + lax.ppermute(part, "docs", pairs)
    return terms


def solution(mesh):
    in_specs = (P("groups", "docs"), P(None, "docs"))
    out_specs = P(("groups", "docs"), None)
    return jax.shard_map(local, mesh=mesh, in_specs=in_specs, out_specs=out_specs, check_vma=False)
```

```python
import functools
import math

import jax
import jax.numpy as jnp
from jax import lax
from jax.experimental import pallas as pl
from jax.experimental.pallas import tpu as pltpu
from jax.sharding import PartitionSpec as P

EPS = 1e-06
LANES = 128


def phases(chips):
    bits = chips.bit_length() - 1
    pairs = [[0, 3 << b, 1 << b, 2 << b] for b in range(0, bits - 1, 2)]
    return pairs + [[0, 1 << bits - 1]] * (bits % 2)


def relative(chips, slot):
    total = 0
    for offsets in reversed(phases(chips)):
        slot, digit = divmod(slot, len(offsets))
        total ^= offsets[digit]
    return total


def partial_squares(x):
    total = None
    for start in range(0, x.shape[1], LANES):
        part = x[:, start : start + LANES].astype(jnp.float32)
        part = part * part
        total = part if total is None else total + part
    return total


def dots_kernel(chips, cuts, train, query, keep, send, train_v, query_v, doc_part, query_part, sem):
    docs, queries = train.shape[0], query.shape[0]
    half = docs // 2
    rows = half // chips
    me = lax.axis_index("docs")
    core, chip = lax.rem(me, 2), lax.div(me, 2)
    spans = list(zip(cuts[:-1], cuts[1:]))
    copies = []
    for k, (low, high) in enumerate(spans):
        cols = pl.ds(low, high - low)
        pair = [
            pltpu.make_async_copy(train.at[:, cols], train_v.at[:, cols], sem.at[k, 0]),
            pltpu.make_async_copy(query.at[:, cols], query_v.at[:, cols], sem.at[k, 1]),
        ]
        for copy in pair:
            copy.start()
        copies.append(pair)
    starts = []
    for owner in (core, 1 - core):
        for slot in range(chips):
            target = jnp.bitwise_xor(chip, relative(chips, slot))
            starts.append(pl.multiple_of(target * (2 * rows) + owner * rows, rows))
    for k, (low, high) in enumerate(spans):
        for copy in copies[k]:
            copy.wait()
        a = jnp.concatenate([train_v[pl.ds(start, rows), low:high] for start in starts], axis=0)
        b = query_v[:, low:high]
        dots = lax.dot_general(b, a, (((1,), (1,)), ((), ())), preferred_element_type=jnp.float32)
        if k == 0:
            keep[:queries, :] = dots[:, :half]
            send[:queries, :] = dots[:, half:]
            doc_part[...] = partial_squares(a)
            query_part[...] = partial_squares(b)
        else:
            keep[:queries, :] += dots[:, :half]
            send[:queries, :] += dots[:, half:]
            doc_part[...] += partial_squares(a)
            query_part[...] += partial_squares(b)
    doc_row = jnp.sum(doc_part[...].T, axis=0, keepdims=True)
    keep[queries : queries + 1, :] = doc_row[:, :half]
    send[queries : queries + 1, :] = doc_row[:, half:]
    query_row = jnp.sum(query_part[...].T, axis=0, keepdims=True)
    for i, low in enumerate(range(0, queries, half)):
        part = query_row[:, low : low + half]
        for out in (keep, send):
            out[queries + 1 + i : queries + 2 + i, : part.shape[1]] = part


def scale_kernel(factor, queries, keep, got, terms):
    half = keep.shape[1]
    doc = lax.rsqrt(keep[queries : queries + 1, :] + got[queries : queries + 1, :] + EPS) * factor
    parts = []
    for i, low in enumerate(range(0, queries, half)):
        row, width = queries + 1 + i, min(half, queries - low)
        parts.append(keep[row : row + 1, :width] + got[row : row + 1, :width])
    query = lax.rsqrt(jnp.concatenate(parts, axis=1) + EPS)
    terms[...] = ((keep[:queries, :] + got[:queries, :]) * doc).T * query


def local(train_grads, query_grads):
    devices = lax.axis_size("docs")
    chips = devices // 2
    docs, width = train_grads.shape
    queries = query_grads.shape[0]
    factor = math.sqrt(2 * width / chips)
    half = docs // 2
    height = pl.cdiv(queries + 1 + pl.cdiv(queries, half), 8) * 8
    packed = jax.ShapeDtypeStruct((height, half), jnp.float32)
    cuts = [0, width // 4, width * 5 // 8, width]
    keep, send = pl.pallas_call(
        functools.partial(dots_kernel, chips, cuts),
        out_shape=[packed, packed],
        in_specs=[pl.BlockSpec(memory_space=pl.ANY)] * 2,
        out_specs=[pl.BlockSpec(memory_space=pltpu.VMEM)] * 2,
        scratch_shapes=[
            pltpu.VMEM((docs, width), jnp.bfloat16),
            pltpu.VMEM((queries, width), jnp.bfloat16),
            pltpu.VMEM((docs, LANES), jnp.float32),
            pltpu.VMEM((queries, LANES), jnp.float32),
            pltpu.SemaphoreType.DMA((len(cuts) - 1, 2)),
        ],
        compiler_params=pltpu.CompilerParams(vmem_limit_bytes=40 * 2**20),
        name="dots",
    )(*(pltpu.with_memory_space_constraint(x, pltpu.HBM) for x in (train_grads, query_grads)))
    got = lax.ppermute(send, "docs", [(i, i ^ 1) for i in range(devices)])
    terms = pl.pallas_call(
        functools.partial(scale_kernel, factor, queries),
        out_shape=jax.ShapeDtypeStruct((half, queries), jnp.float32),
        compiler_params=pltpu.CompilerParams(vmem_limit_bytes=40 * 2**20),
        name="scale",
    )(keep, got)
    for offsets in phases(chips):
        parts = jnp.split(terms, len(offsets))
        moves = [[(i, i ^ 2 * offset) for i in range(devices)] for offset in offsets]
        terms = parts[0]
        for part, pairs in zip(parts[1:], moves[1:]):
            terms = terms + lax.ppermute(part, "docs", pairs)
    return terms


def solution(mesh):
    in_specs = (P("groups", "docs"), P(None, "docs"))
    out_specs = P(("groups", "docs"), None)
    return jax.shard_map(local, mesh=mesh, in_specs=in_specs, out_specs=out_specs, check_vma=False)
```

```python
import functools
import math

import jax
import jax.numpy as jnp
from jax import lax
from jax.experimental import pallas as pl
from jax.experimental.pallas import tpu as pltpu
from jax.sharding import PartitionSpec as P

EPS = 1e-06
LANES = 128


def phases(chips):
    bits = chips.bit_length() - 1
    pairs = [[0, 3 << b, 1 << b, 2 << b] for b in range(0, bits - 1, 2)]
    return pairs + [[0, 1 << bits - 1]] * (bits % 2)


def relative(chips, slot):
    total = 0
    for offsets in reversed(phases(chips)):
        slot, digit = divmod(slot, len(offsets))
        total ^= offsets[digit]
    return total


def partial_squares(x):
    total = None
    for start in range(0, x.shape[1], LANES):
        part = x[:, start : start + LANES].astype(jnp.float32)
        part = part * part
        total = part if total is None else total + part
    return total


def dots_kernel(chips, cuts, train, query, keep, send, train_v, query_v, doc_part, query_part, sem):
    docs, queries = train.shape[0], query.shape[0]
    half = docs // 2
    rows = half // chips
    me = lax.axis_index("docs")
    core, chip = lax.rem(me, 2), lax.div(me, 2)
    spans = list(zip(cuts[:-1], cuts[1:]))
    copies = []
    for k, (low, high) in enumerate(spans):
        cols = pl.ds(low, high - low)
        pair = [
            pltpu.make_async_copy(train.at[:, cols], train_v.at[:, cols], sem.at[k, 0]),
            pltpu.make_async_copy(query.at[:, cols], query_v.at[:, cols], sem.at[k, 1]),
        ]
        for copy in pair:
            copy.start()
        copies.append(pair)
    middle = pl.cdiv(queries, 32) * 16
    starts = []
    for owner in (core, 1 - core):
        for slot in range(chips):
            target = jnp.bitwise_xor(chip, relative(chips, slot))
            starts.append(pl.multiple_of(target * (2 * rows) + owner * rows, rows))
    for k, (low, high) in enumerate(spans):
        for copy in copies[k]:
            copy.wait()
        a = jnp.concatenate([train_v[pl.ds(start, rows), low:high] for start in starts], axis=0)
        b = query_v[:, low:high]
        for first, end in ((0, middle), (middle, queries)):
            dots = lax.dot_general(b[first:end], a, (((1,), (1,)), ((), ())), preferred_element_type=jnp.float32)
            squares = partial_squares(b[first:end])
            if k == 0:
                keep[first:end, :] = dots[:, :half]
                send[first:end, :] = dots[:, half:]
                query_part[first:end, :] = squares
            else:
                keep[first:end, :] += dots[:, :half]
                send[first:end, :] += dots[:, half:]
                query_part[first:end, :] += squares
        if k == 0:
            doc_part[...] = partial_squares(a)
        else:
            doc_part[...] += partial_squares(a)
    doc_row = jnp.sum(doc_part[...].T, axis=0, keepdims=True)
    keep[queries : queries + 1, :] = doc_row[:, :half]
    send[queries : queries + 1, :] = doc_row[:, half:]
    query_row = jnp.sum(query_part[...].T, axis=0, keepdims=True)
    for i, low in enumerate(range(0, queries, half)):
        part = query_row[:, low : low + half]
        for out in (keep, send):
            out[queries + 1 + i : queries + 2 + i, : part.shape[1]] = part


def scale_kernel(factor, queries, keep, got, terms):
    half = keep.shape[1]
    doc = lax.rsqrt(keep[queries : queries + 1, :] + got[queries : queries + 1, :] + EPS) * factor
    parts = []
    for i, low in enumerate(range(0, queries, half)):
        row, width = queries + 1 + i, min(half, queries - low)
        parts.append(keep[row : row + 1, :width] + got[row : row + 1, :width])
    query = lax.rsqrt(jnp.concatenate(parts, axis=1) + EPS)
    terms[...] = ((keep[:queries, :] + got[:queries, :]) * doc).T * query


def local(train_grads, query_grads):
    devices = lax.axis_size("docs")
    chips = devices // 2
    docs, width = train_grads.shape
    queries = query_grads.shape[0]
    factor = math.sqrt(2 * width / chips)
    half = docs // 2
    height = pl.cdiv(queries + 1 + pl.cdiv(queries, half), 8) * 8
    packed = jax.ShapeDtypeStruct((height, half), jnp.float32)
    cuts = [0, width // 4, width * 5 // 8, width]
    keep, send = pl.pallas_call(
        functools.partial(dots_kernel, chips, cuts),
        out_shape=[packed, packed],
        in_specs=[pl.BlockSpec(memory_space=pl.ANY)] * 2,
        out_specs=[pl.BlockSpec(memory_space=pltpu.VMEM)] * 2,
        scratch_shapes=[
            pltpu.VMEM((docs, width), jnp.bfloat16),
            pltpu.VMEM((queries, width), jnp.bfloat16),
            pltpu.VMEM((docs, LANES), jnp.float32),
            pltpu.VMEM((queries, LANES), jnp.float32),
            pltpu.SemaphoreType.DMA((len(cuts) - 1, 2)),
        ],
        compiler_params=pltpu.CompilerParams(vmem_limit_bytes=40 * 2**20),
        name="dots",
    )(*(pltpu.with_memory_space_constraint(x, pltpu.HBM) for x in (train_grads, query_grads)))
    got = lax.ppermute(send, "docs", [(i, i ^ 1) for i in range(devices)])
    terms = pl.pallas_call(
        functools.partial(scale_kernel, factor, queries),
        out_shape=jax.ShapeDtypeStruct((half, queries), jnp.float32),
        compiler_params=pltpu.CompilerParams(vmem_limit_bytes=40 * 2**20),
        name="scale",
    )(keep, got)
    for offsets in phases(chips):
        parts = jnp.split(terms, len(offsets))
        moves = [[(i, i ^ 2 * offset) for i in range(devices)] for offset in offsets]
        terms = parts[0]
        for part, pairs in zip(parts[1:], moves[1:]):
            terms = terms + lax.ppermute(part, "docs", pairs)
    return terms


def solution(mesh):
    in_specs = (P("groups", "docs"), P(None, "docs"))
    out_specs = P(("groups", "docs"), None)
    return jax.shard_map(local, mesh=mesh, in_specs=in_specs, out_specs=out_specs, check_vma=False)
```

```python
import functools
import math

import jax
import jax.numpy as jnp
from jax import lax
from jax.experimental import pallas as pl
from jax.experimental.pallas import tpu as pltpu
from jax.sharding import PartitionSpec as P

EPS = 1e-06
LANES = 128


def phases(chips):
    bits = chips.bit_length() - 1
    fours = [(2 << b, [(0, 0), (2 << b, 3 << b), (3 << b, 2 << b), (1 << b, 1 << b)]) for b in range(0, bits - 1, 2)]
    last = 1 << bits - 1
    return fours + [(last, [(0, 0), (last, last)])] * (bits % 2)


def owner_of(chips, chip, slot):
    result = chip
    for mask, offsets in reversed(phases(chips)):
        slot, digit = divmod(slot, len(offsets))
        clear, marked = offsets[digit]
        result = jnp.bitwise_xor(result, jnp.where(jnp.bitwise_and(chip, mask) == 0, clear, marked))
    return result


def partial_squares(x):
    total = None
    for start in range(0, x.shape[1], LANES):
        part = x[:, start : start + LANES].astype(jnp.float32)
        part = part * part
        total = part if total is None else total + part
    return total


def dots_kernel(chips, cuts, train, query, keep, send, train_v, query_v, doc_part, query_part, sem):
    docs, queries = train.shape[0], query.shape[0]
    half = docs // 2
    rows = half // chips
    me = lax.axis_index("docs")
    core, chip = lax.rem(me, 2), lax.div(me, 2)
    spans = list(zip(cuts[:-1], cuts[1:]))
    copies = []
    for k, (low, high) in enumerate(spans):
        cols = pl.ds(low, high - low)
        pair = [
            pltpu.make_async_copy(train.at[:, cols], train_v.at[:, cols], sem.at[k, 0]),
            pltpu.make_async_copy(query.at[:, cols], query_v.at[:, cols], sem.at[k, 1]),
        ]
        for copy in pair:
            copy.start()
        copies.append(pair)
    middle = pl.cdiv(queries, 32) * 16
    starts = []
    for owner in (core, 1 - core):
        for slot in range(chips):
            starts.append(pl.multiple_of(owner_of(chips, chip, slot) * (2 * rows) + owner * rows, rows))
    for k, (low, high) in enumerate(spans):
        for copy in copies[k]:
            copy.wait()
        a = jnp.concatenate([train_v[pl.ds(start, rows), low:high] for start in starts], axis=0)
        b = query_v[:, low:high]
        for first, end in ((0, middle), (middle, queries)):
            dots = lax.dot_general(b[first:end], a, (((1,), (1,)), ((), ())), preferred_element_type=jnp.float32)
            squares = partial_squares(b[first:end])
            if k == 0:
                keep[first:end, :] = dots[:, :half]
                send[first:end, :] = dots[:, half:]
                query_part[first:end, :] = squares
            else:
                keep[first:end, :] += dots[:, :half]
                send[first:end, :] += dots[:, half:]
                query_part[first:end, :] += squares
        if k == 0:
            doc_part[...] = partial_squares(a)
        else:
            doc_part[...] += partial_squares(a)
    doc_row = jnp.sum(doc_part[...].T, axis=0, keepdims=True)
    keep[queries : queries + 1, :] = doc_row[:, :half]
    send[queries : queries + 1, :] = doc_row[:, half:]
    query_row = jnp.sum(query_part[...].T, axis=0, keepdims=True)
    for i, low in enumerate(range(0, queries, half)):
        part = query_row[:, low : low + half]
        for out in (keep, send):
            out[queries + 1 + i : queries + 2 + i, : part.shape[1]] = part


def scale_kernel(factor, queries, keep, got, *terms):
    half = keep.shape[1]
    doc = lax.rsqrt(keep[queries : queries + 1, :] + got[queries : queries + 1, :] + EPS) * factor
    parts = []
    for i, low in enumerate(range(0, queries, half)):
        row, width = queries + 1 + i, min(half, queries - low)
        parts.append(keep[row : row + 1, :width] + got[row : row + 1, :width])
    query = lax.rsqrt(jnp.concatenate(parts, axis=1) + EPS)
    total = ((keep[:queries, :] + got[:queries, :]) * doc).T * query
    size = terms[0].shape[0]
    for i, part in enumerate(terms):
        part[...] = total[i * size : (i + 1) * size, :]


def local(train_grads, query_grads):
    devices = lax.axis_size("docs")
    chips = devices // 2
    docs, width = train_grads.shape
    queries = query_grads.shape[0]
    factor = math.sqrt(2 * width / chips)
    half = docs // 2
    height = pl.cdiv(queries + 1 + pl.cdiv(queries, half), 8) * 8
    packed = jax.ShapeDtypeStruct((height, half), jnp.float32)
    cuts = [0, width // 4, width * 5 // 8, width]
    keep, send = pl.pallas_call(
        functools.partial(dots_kernel, chips, cuts),
        out_shape=[packed, packed],
        in_specs=[pl.BlockSpec(memory_space=pl.ANY)] * 2,
        out_specs=[pl.BlockSpec(memory_space=pltpu.VMEM)] * 2,
        scratch_shapes=[
            pltpu.VMEM((docs, width), jnp.bfloat16),
            pltpu.VMEM((queries, width), jnp.bfloat16),
            pltpu.VMEM((docs, LANES), jnp.float32),
            pltpu.VMEM((queries, LANES), jnp.float32),
            pltpu.SemaphoreType.DMA((len(cuts) - 1, 2)),
        ],
        compiler_params=pltpu.CompilerParams(vmem_limit_bytes=40 * 2**20),
        name="dots",
    )(*(pltpu.with_memory_space_constraint(x, pltpu.HBM) for x in (train_grads, query_grads)))
    got = lax.ppermute(send, "docs", [(i, i ^ 1) for i in range(devices)])
    exchanges = phases(chips)
    count = len(exchanges[0][1])
    parts = pl.pallas_call(
        functools.partial(scale_kernel, factor, queries),
        out_shape=[jax.ShapeDtypeStruct((half // count, queries), jnp.float32)] * count,
        compiler_params=pltpu.CompilerParams(vmem_limit_bytes=40 * 2**20),
        name="scale",
    )(keep, got)
    for i, (mask, offsets) in enumerate(exchanges):
        if i > 0:
            parts = jnp.split(terms, len(offsets))
        terms = parts[0]
        for part, (clear, marked) in zip(parts[1:], offsets[1:]):
            pairs = [(d, d ^ 2 * (marked if d // 2 & mask else clear)) for d in range(devices)]
            terms = terms + lax.ppermute(part, "docs", pairs)
    return terms


def solution(mesh):
    in_specs = (P("groups", "docs"), P(None, "docs"))
    out_specs = P(("groups", "docs"), None)
    return jax.shard_map(local, mesh=mesh, in_specs=in_specs, out_specs=out_specs, check_vma=False)
```

```python
import functools
import math

import jax
import jax.numpy as jnp
from jax import lax
from jax.experimental import pallas as pl
from jax.experimental.pallas import tpu as pltpu
from jax.sharding import PartitionSpec as P

EPS = 1e-06
LANES = 128


def split_bits(chips):
    bits = chips.bit_length() - 1
    return list(range(0, bits - 1, 2)), bits % 2


def offsets(chips, b, chip):
    parity = ((chip >> b) ^ (chip >> (b + 1))) & 1
    near = (2 - parity, 1 + parity, 3)
    far = (3, 2, 1)
    is_far = (chip >> (chips.bit_length() - 2)) & 1 if split_bits(chips)[1] else 0
    return [0] + [(n + is_far * (f - n)) << b for n, f in zip(near, far)]


def owner_of(chips, chip, slot):
    fours, pair = split_bits(chips)
    result = chip
    if pair:
        slot, digit = divmod(slot, 2)
        result = result ^ (digit * (chips // 2))
    for b in reversed(fours):
        slot, digit = divmod(slot, 4)
        result = result ^ offsets(chips, b, chip)[digit]
    return result


def partial_squares(x):
    total = None
    for start in range(0, x.shape[1], LANES):
        part = x[:, start : start + LANES].astype(jnp.float32)
        part = part * part
        total = part if total is None else total + part
    return total


def dots_kernel(chips, cuts, train, query, keep, send, train_v, query_v, doc_part, query_part, sem):
    docs, queries = train.shape[0], query.shape[0]
    half = docs // 2
    rows = half // chips
    me = lax.axis_index("docs")
    core, chip = lax.rem(me, 2), lax.div(me, 2)
    spans = list(zip(cuts[:-1], cuts[1:]))
    copies = []
    for k, (low, high) in enumerate(spans):
        cols = pl.ds(low, high - low)
        pair = [
            pltpu.make_async_copy(train.at[:, cols], train_v.at[:, cols], sem.at[k, 0]),
            pltpu.make_async_copy(query.at[:, cols], query_v.at[:, cols], sem.at[k, 1]),
        ]
        for copy in pair:
            copy.start()
        copies.append(pair)
    middle = pl.cdiv(queries, 32) * 16
    starts = []
    for owner in (core, 1 - core):
        for slot in range(chips):
            starts.append(pl.multiple_of(owner_of(chips, chip, slot) * (2 * rows) + owner * rows, rows))
    for k, (low, high) in enumerate(spans):
        for copy in copies[k]:
            copy.wait()
        a = jnp.concatenate([train_v[pl.ds(start, rows), low:high] for start in starts], axis=0)
        b = query_v[:, low:high]
        for first, end in ((0, middle), (middle, queries)):
            dots = lax.dot_general(b[first:end], a, (((1,), (1,)), ((), ())), preferred_element_type=jnp.float32)
            squares = partial_squares(b[first:end])
            if k == 0:
                keep[first:end, :] = dots[:, :half]
                send[first:end, :] = dots[:, half:]
                query_part[first:end, :] = squares
            else:
                keep[first:end, :] += dots[:, :half]
                send[first:end, :] += dots[:, half:]
                query_part[first:end, :] += squares
        if k == 0:
            doc_part[...] = partial_squares(a)
        else:
            doc_part[...] += partial_squares(a)
    doc_row = jnp.sum(doc_part[...].T, axis=0, keepdims=True)
    keep[queries : queries + 1, :] = doc_row[:, :half]
    send[queries : queries + 1, :] = doc_row[:, half:]
    query_row = jnp.sum(query_part[...].T, axis=0, keepdims=True)
    for i, low in enumerate(range(0, queries, half)):
        part = query_row[:, low : low + half]
        for out in (keep, send):
            out[queries + 1 + i : queries + 2 + i, : part.shape[1]] = part


def scale_kernel(factor, queries, keep, got, *terms):
    half = keep.shape[1]
    doc = lax.rsqrt(keep[queries : queries + 1, :] + got[queries : queries + 1, :] + EPS) * factor
    parts = []
    for i, low in enumerate(range(0, queries, half)):
        row, width = queries + 1 + i, min(half, queries - low)
        parts.append(keep[row : row + 1, :width] + got[row : row + 1, :width])
    query = lax.rsqrt(jnp.concatenate(parts, axis=1) + EPS)
    total = ((keep[:queries, :] + got[:queries, :]) * doc).T * query
    size = terms[0].shape[0]
    for i, part in enumerate(terms):
        part[...] = total[i * size : (i + 1) * size, :]


def local(train_grads, query_grads):
    devices = lax.axis_size("docs")
    chips = devices // 2
    docs, width = train_grads.shape
    queries = query_grads.shape[0]
    factor = math.sqrt(2 * width / chips)
    half = docs // 2
    height = pl.cdiv(queries + 1 + pl.cdiv(queries, half), 8) * 8
    packed = jax.ShapeDtypeStruct((height, half), jnp.float32)
    cuts = [0, width // 4, width * 5 // 8, width]
    keep, send = pl.pallas_call(
        functools.partial(dots_kernel, chips, cuts),
        out_shape=[packed, packed],
        in_specs=[pl.BlockSpec(memory_space=pl.ANY)] * 2,
        out_specs=[pl.BlockSpec(memory_space=pltpu.VMEM)] * 2,
        scratch_shapes=[
            pltpu.VMEM((docs, width), jnp.bfloat16),
            pltpu.VMEM((queries, width), jnp.bfloat16),
            pltpu.VMEM((docs, LANES), jnp.float32),
            pltpu.VMEM((queries, LANES), jnp.float32),
            pltpu.SemaphoreType.DMA((len(cuts) - 1, 2)),
        ],
        compiler_params=pltpu.CompilerParams(vmem_limit_bytes=40 * 2**20),
        name="dots",
    )(*(pltpu.with_memory_space_constraint(x, pltpu.HBM) for x in (train_grads, query_grads)))
    got = lax.ppermute(send, "docs", [(i, i ^ 1) for i in range(devices)])
    fours, pair = split_bits(chips)
    count = 4 if fours else 2
    parts = pl.pallas_call(
        functools.partial(scale_kernel, factor, queries),
        out_shape=[jax.ShapeDtypeStruct((half // count, queries), jnp.float32)] * count,
        compiler_params=pltpu.CompilerParams(vmem_limit_bytes=40 * 2**20),
        name="scale",
    )(keep, got)

    def move(part, b, i):
        pairs = [(d, d ^ 2 * offsets(chips, b, d // 2)[i]) for d in range(devices)]
        return lax.ppermute(part, "docs", pairs)

    def cross(part):
        return lax.ppermute(part, "docs", [(d, d ^ chips) for d in range(devices)])

    for b in fours:
        if b > 0:
            parts = jnp.split(terms, 4)
        if pair and b == fours[-1]:
            size = parts[0].shape[0] // 2
            first, second = move(parts[1], b, 1), move(parts[2], b, 2)
            third_far = move(parts[3][size:], b, 3)
            third_near = move(parts[3][:size], b, 3)
            far = parts[0][size:] + first[size:] + second[size:] + third_far
            return parts[0][:size] + first[:size] + second[:size] + third_near + cross(far)
        terms = parts[0] + move(parts[1], b, 1) + move(parts[2], b, 2) + move(parts[3], b, 3)
    if pair:
        terms = parts[0] + cross(parts[1])
    return terms


def solution(mesh):
    in_specs = (P("groups", "docs"), P(None, "docs"))
    out_specs = P(("groups", "docs"), None)
    return jax.shard_map(local, mesh=mesh, in_specs=in_specs, out_specs=out_specs, check_vma=False)
```

```python
import functools
import math

import jax
import jax.numpy as jnp
from jax import lax
from jax.experimental import pallas as pl
from jax.experimental.pallas import tpu as pltpu
from jax.sharding import PartitionSpec as P

EPS = 1e-06
LANES = 128


def split_bits(chips):
    bits = chips.bit_length() - 1
    return list(range(0, bits - 1, 2)), bits % 2


def offsets(b, chip):
    parity = ((chip >> b) ^ (chip >> (b + 1))) & 1
    return [0] + [offset << b for offset in (2 - parity, 1 + parity, 3)]


def owner_of(chips, chip, slot):
    fours, pair = split_bits(chips)
    result = chip
    if pair:
        slot, digit = divmod(slot, 2)
        result = result ^ (digit * (chips // 2))
    for b in reversed(fours):
        slot, digit = divmod(slot, 4)
        result = result ^ offsets(b, chip)[digit]
    return result


def partial_squares(x):
    total = None
    for start in range(0, x.shape[1], LANES):
        part = x[:, start : start + LANES].astype(jnp.float32)
        part = part * part
        total = part if total is None else total + part
    return total


def dots_kernel(chips, cuts, train, query, keep, send, train_v, query_v, doc_part, query_part, sem):
    docs, queries = train.shape[0], query.shape[0]
    half = docs // 2
    rows = half // chips
    me = lax.axis_index("docs")
    core, chip = lax.rem(me, 2), lax.div(me, 2)
    spans = list(zip(cuts[:-1], cuts[1:]))
    copies = []
    for k, (low, high) in enumerate(spans):
        cols = pl.ds(low, high - low)
        pair = [
            pltpu.make_async_copy(train.at[:, cols], train_v.at[:, cols], sem.at[k, 0]),
            pltpu.make_async_copy(query.at[:, cols], query_v.at[:, cols], sem.at[k, 1]),
        ]
        for copy in pair:
            copy.start()
        copies.append(pair)
    middle = pl.cdiv(queries, 32) * 16
    starts = []
    for owner in (core, 1 - core):
        for slot in range(chips):
            starts.append(pl.multiple_of(owner_of(chips, chip, slot) * (2 * rows) + owner * rows, rows))
    for k, (low, high) in enumerate(spans):
        for copy in copies[k]:
            copy.wait()
        a = jnp.concatenate([train_v[pl.ds(start, rows), low:high] for start in starts], axis=0)
        b = query_v[:, low:high]
        for first, end in ((0, middle), (middle, queries)):
            dots = lax.dot_general(b[first:end], a, (((1,), (1,)), ((), ())), preferred_element_type=jnp.float32)
            squares = partial_squares(b[first:end])
            if k == 0:
                keep[first:end, :] = dots[:, :half]
                send[first:end, :] = dots[:, half:]
                query_part[first:end, :] = squares
            else:
                keep[first:end, :] += dots[:, :half]
                send[first:end, :] += dots[:, half:]
                query_part[first:end, :] += squares
        if k == 0:
            doc_part[...] = partial_squares(a)
        else:
            doc_part[...] += partial_squares(a)
    doc_row = jnp.sum(doc_part[...].T, axis=0, keepdims=True)
    keep[queries : queries + 1, :] = doc_row[:, :half]
    send[queries : queries + 1, :] = doc_row[:, half:]
    query_row = jnp.sum(query_part[...].T, axis=0, keepdims=True)
    for i, low in enumerate(range(0, queries, half)):
        part = query_row[:, low : low + half]
        for out in (keep, send):
            out[queries + 1 + i : queries + 2 + i, : part.shape[1]] = part


def scale_kernel(factor, queries, keep, got, *terms):
    half = keep.shape[1]
    doc = lax.rsqrt(keep[queries : queries + 1, :] + got[queries : queries + 1, :] + EPS) * factor
    parts = []
    for i, low in enumerate(range(0, queries, half)):
        row, width = queries + 1 + i, min(half, queries - low)
        parts.append(keep[row : row + 1, :width] + got[row : row + 1, :width])
    query = lax.rsqrt(jnp.concatenate(parts, axis=1) + EPS)
    total = ((keep[:queries, :] + got[:queries, :]) * doc).T * query
    size = terms[0].shape[0]
    for i, part in enumerate(terms):
        part[...] = total[i * size : (i + 1) * size, :]


def local(train_grads, query_grads):
    devices = lax.axis_size("docs")
    chips = devices // 2
    docs, width = train_grads.shape
    queries = query_grads.shape[0]
    factor = math.sqrt(2 * width / chips)
    half = docs // 2
    height = pl.cdiv(queries + 1 + pl.cdiv(queries, half), 8) * 8
    packed = jax.ShapeDtypeStruct((height, half), jnp.float32)
    cuts = [0, width // 4, width * 5 // 8, width]
    keep, send = pl.pallas_call(
        functools.partial(dots_kernel, chips, cuts),
        out_shape=[packed, packed],
        in_specs=[pl.BlockSpec(memory_space=pl.ANY)] * 2,
        out_specs=[pl.BlockSpec(memory_space=pltpu.VMEM)] * 2,
        scratch_shapes=[
            pltpu.VMEM((docs, width), jnp.bfloat16),
            pltpu.VMEM((queries, width), jnp.bfloat16),
            pltpu.VMEM((docs, LANES), jnp.float32),
            pltpu.VMEM((queries, LANES), jnp.float32),
            pltpu.SemaphoreType.DMA((len(cuts) - 1, 2)),
        ],
        compiler_params=pltpu.CompilerParams(vmem_limit_bytes=40 * 2**20),
        name="dots",
    )(*(pltpu.with_memory_space_constraint(x, pltpu.HBM) for x in (train_grads, query_grads)))
    got = lax.ppermute(send, "docs", [(i, i ^ 1) for i in range(devices)])
    fours, pair = split_bits(chips)
    count = 4 if fours else 2
    parts = pl.pallas_call(
        functools.partial(scale_kernel, factor, queries),
        out_shape=[jax.ShapeDtypeStruct((half // count, queries), jnp.float32)] * count,
        compiler_params=pltpu.CompilerParams(vmem_limit_bytes=40 * 2**20),
        name="scale",
    )(keep, got)

    def move(part, b, i):
        pairs = [(d, d ^ 2 * offsets(b, d // 2)[i]) for d in range(devices)]
        return lax.ppermute(part, "docs", pairs)

    def cross(part):
        return lax.ppermute(part, "docs", [(d, d ^ chips) for d in range(devices)])

    for b in fours:
        if b > 0:
            parts = jnp.split(terms, 4)
        if pair and b == fours[-1]:
            size = parts[0].shape[0] // 2
            first, second = move(parts[1], b, 1), move(parts[2], b, 2)
            third_far = move(parts[3][size:], b, 3)
            third_near = move(parts[3][:size], b, 3)
            far = parts[0][size:] + first[size:] + second[size:] + third_far
            return parts[0][:size] + first[:size] + second[:size] + third_near + cross(far)
        terms = parts[0] + move(parts[1], b, 1) + move(parts[2], b, 2) + move(parts[3], b, 3)
    if pair:
        terms = parts[0] + cross(parts[1])
    return terms


def solution(mesh):
    in_specs = (P("groups", "docs"), P(None, "docs"))
    out_specs = P(("groups", "docs"), None)
    return jax.shard_map(local, mesh=mesh, in_specs=in_specs, out_specs=out_specs, check_vma=False)
```

```python
import functools
import math

import jax
import jax.numpy as jnp
from jax import lax
from jax.experimental import pallas as pl
from jax.experimental.pallas import tpu as pltpu
from jax.sharding import PartitionSpec as P

EPS = 1e-06
LANES = 128


def split_bits(chips):
    bits = chips.bit_length() - 1
    return list(range(0, bits - 1, 2)), bits % 2


def offsets(b, chip):
    parity = ((chip >> b) ^ (chip >> (b + 1))) & 1
    return [0] + [offset << b for offset in (2 - parity, 1 + parity, 3)]


def owner_of(chips, chip, slot):
    fours, pair = split_bits(chips)
    result = chip
    if pair:
        slot, digit = divmod(slot, 2)
        result = result ^ (digit * (chips // 2))
    for b in reversed(fours):
        slot, digit = divmod(slot, 4)
        result = result ^ offsets(b, chip)[digit]
    return result


def partial_squares(x):
    total = None
    for start in range(0, x.shape[1], LANES):
        part = x[:, start : start + LANES].astype(jnp.float32)
        part = part * part
        total = part if total is None else total + part
    return total


def dots_kernel(chips, cuts, train, query, keep, send, train_v, query_v, doc_part, query_part, sem):
    docs, queries = train.shape[0], query.shape[0]
    half = docs // 2
    rows = half // chips
    me = lax.axis_index("docs")
    core, chip = lax.rem(me, 2), lax.div(me, 2)
    spans = list(zip(cuts[:-1], cuts[1:]))
    copies = []
    for k, (low, high) in enumerate(spans):
        cols = pl.ds(low, high - low)
        pair = [
            pltpu.make_async_copy(train.at[:, cols], train_v.at[:, cols], sem.at[k, 0]),
            pltpu.make_async_copy(query.at[:, cols], query_v.at[:, cols], sem.at[k, 1]),
        ]
        for copy in pair:
            copy.start()
        copies.append(pair)
    middle = pl.cdiv(queries, 32) * 16
    starts = []
    for owner in (core, 1 - core):
        for slot in range(chips):
            starts.append(pl.multiple_of(owner_of(chips, chip, slot) * (2 * rows) + owner * rows, rows))
    for k, (low, high) in enumerate(spans):
        for copy in copies[k]:
            copy.wait()
        a = jnp.concatenate([train_v[pl.ds(start, rows), low:high] for start in starts], axis=0)
        b = query_v[:, low:high]
        for first, end in ((0, middle), (middle, queries)):
            dots = lax.dot_general(b[first:end], a, (((1,), (1,)), ((), ())), preferred_element_type=jnp.float32)
            squares = partial_squares(b[first:end])
            if k == 0:
                keep[first:end, :] = dots[:, :half]
                send[first:end, :] = dots[:, half:]
                query_part[first:end, :] = squares
            else:
                keep[first:end, :] += dots[:, :half]
                send[first:end, :] += dots[:, half:]
                query_part[first:end, :] += squares
        if k == 0:
            doc_part[...] = partial_squares(a)
        else:
            doc_part[...] += partial_squares(a)
    doc_row = jnp.sum(doc_part[...].T, axis=0, keepdims=True)
    keep[queries : queries + 1, :] = doc_row[:, :half]
    send[queries : queries + 1, :] = doc_row[:, half:]
    query_row = jnp.sum(query_part[...].T, axis=0, keepdims=True)
    for i, low in enumerate(range(0, queries, half)):
        part = query_row[:, low : low + half]
        for out in (keep, send):
            out[queries + 1 + i : queries + 2 + i, : part.shape[1]] = part


def scale_kernel(factor, queries, keep, got, *terms):
    half = keep.shape[1]
    doc = lax.rsqrt(keep[queries : queries + 1, :] + got[queries : queries + 1, :] + EPS) * factor
    parts = []
    for i, low in enumerate(range(0, queries, half)):
        row, width = queries + 1 + i, min(half, queries - low)
        parts.append(keep[row : row + 1, :width] + got[row : row + 1, :width])
    query = lax.rsqrt(jnp.concatenate(parts, axis=1) + EPS)
    total = ((keep[:queries, :] + got[:queries, :]) * doc).T * query
    low = 0
    for part in terms:
        part[...] = total[low : low + part.shape[0], :]
        low += part.shape[0]


def local(train_grads, query_grads):
    devices = lax.axis_size("docs")
    chips = devices // 2
    docs, width = train_grads.shape
    queries = query_grads.shape[0]
    factor = math.sqrt(2 * width / chips)
    half = docs // 2
    height = pl.cdiv(queries + 1 + pl.cdiv(queries, half), 8) * 8
    packed = jax.ShapeDtypeStruct((height, half), jnp.float32)
    cuts = [0, width // 4, width * 5 // 8, width]
    keep, send = pl.pallas_call(
        functools.partial(dots_kernel, chips, cuts),
        out_shape=[packed, packed],
        in_specs=[pl.BlockSpec(memory_space=pl.ANY)] * 2,
        out_specs=[pl.BlockSpec(memory_space=pltpu.VMEM)] * 2,
        scratch_shapes=[
            pltpu.VMEM((docs, width), jnp.bfloat16),
            pltpu.VMEM((queries, width), jnp.bfloat16),
            pltpu.VMEM((docs, LANES), jnp.float32),
            pltpu.VMEM((queries, LANES), jnp.float32),
            pltpu.SemaphoreType.DMA((len(cuts) - 1, 2)),
        ],
        compiler_params=pltpu.CompilerParams(vmem_limit_bytes=40 * 2**20),
        name="dots",
    )(*(pltpu.with_memory_space_constraint(x, pltpu.HBM) for x in (train_grads, query_grads)))
    got = lax.ppermute(send, "docs", [(i, i ^ 1) for i in range(devices)])
    fours, pair = split_bits(chips)
    count = 4 if fours else 2
    heights = [half // count] * count
    if pair and len(fours) == 1:
        heights = heights[:-1] + [half // count // 2] * 2
    parts = pl.pallas_call(
        functools.partial(scale_kernel, factor, queries),
        out_shape=[jax.ShapeDtypeStruct((r, queries), jnp.float32) for r in heights],
        compiler_params=pltpu.CompilerParams(vmem_limit_bytes=40 * 2**20),
        name="scale",
    )(keep, got)

    def move(part, b, i):
        pairs = [(d, d ^ 2 * offsets(b, d // 2)[i]) for d in range(devices)]
        return lax.ppermute(part, "docs", pairs)

    def cross(part):
        return lax.ppermute(part, "docs", [(d, d ^ chips) for d in range(devices)])

    for b in fours:
        if b > 0:
            parts = jnp.split(terms, 4)
        if pair and b == fours[-1]:
            size = parts[0].shape[0] // 2
            last = parts[3:] if len(parts) == 5 else [parts[3][:size], parts[3][size:]]
            first, second = move(parts[1], b, 1), move(parts[2], b, 2)
            third_far = move(last[1], b, 3)
            third_near = move(last[0], b, 3)
            far = parts[0][size:] + first[size:] + second[size:] + third_far
            return parts[0][:size] + first[:size] + second[:size] + third_near + cross(far)
        terms = parts[0] + move(parts[1], b, 1) + move(parts[2], b, 2) + move(parts[3], b, 3)
    if pair:
        terms = parts[0] + cross(parts[1])
    return terms


def solution(mesh):
    in_specs = (P("groups", "docs"), P(None, "docs"))
    out_specs = P(("groups", "docs"), None)
    return jax.shard_map(local, mesh=mesh, in_specs=in_specs, out_specs=out_specs, check_vma=False)
```
